256 devices in a mesh: gx: 4 (over x), gy: 8 (over z), gz: 8 (over y, core).
Axes of the slice: x: 4, y: 4, z: 8, core: 2. Of those that a mesh axis runs over, the one named last changes fastest.
Arguments:
- multipoles: bfloat16 [65536, 256], P(('gx', 'gy', 'gz')), may hold values from -6 to 6
- translations: bfloat16 [16, 256, 256], replicated, may hold values from -0.09375 to 0.09375
- send_index: int32 [256, 256, 2], P(('gx', 'gy', 'gz')), may hold values from 0 to 255
- far_slots: int32 [65536, 16], P(('gx', 'gy', 'gz')), may hold values from 0 to 511
- far_types: int32 [65536, 16], P(('gx', 'gy', 'gz')), may hold values from 0 to 15
- near_list: int32 [65536, 8], P(('gx', 'gy', 'gz')), may hold values from 0 to 287
- particles: float32 [65536, 6, 128], P(('gx', 'gy', 'gz')), may hold values from -4 to 4
Outputs:
- local_expansions: float32 [65536, 256], P(('gx', 'gy', 'gz'))
- velocities: float32 [65536, 3, 128], P(('gx', 'gy', 'gz'))
The draws below stay inside these ranges and needn't reach their ends.
All inputs are finite; a program needn't handle non-finite values.
Results may differ from the reference program's by a relative error of at most 0.0024.
Values may be sent and summed in bfloat16 or wider, within the bound.
No kernel may reach another device: no remote copies, remote signals or barrier semaphores. Data moves between devices by JAX's collectives and lax.ppermute only.
A program may use at most 64 MiB of HBM per device.

```python
import jax
import jax.numpy as jnp
from jax import lax

Q = 256
P_SIZE = 128
LEAF_DEV = 256
NT = 16
NL = 16
NN = 8
CAP = 2
HALO = 16
LEAVES = 65536
SLOTS = 512
DEVICES = 256


def plant(array, key, low, largest):
    longest = array.shape.index(max(array.shape))
    spots = []
    for shift in (0, 1):
        where = [jax.random.randint(jax.random.fold_in(key, axis), (), 0, length) for axis, length in enumerate(array.shape)]
        where[longest] = (where[longest] + shift) % array.shape[longest]
        spots.append(tuple(where))
    return array.at[spots[0]].set(low).at[spots[1]].set(largest)


def level_of(own_key, dims, split, low, largest):
    def one(dim, blocks):
        draws = jax.random.uniform(jax.random.fold_in(jax.random.fold_in(own_key, 6), dim), (blocks,), jnp.float32, low / len(split), largest / len(split))
        return jnp.repeat(jnp.exp(draws), dims[dim] // blocks).reshape((-1,) + (1,) * (len(dims) - dim - 1))

    level = one(*split[0])
    for cut in split[1:]:
        level = level * one(*cut)
    return level


def centred(key, extent, deviation, bound, split=(), kind=jnp.bfloat16):
    entries = deviation * jax.random.normal(key, extent, jnp.float32)
    if split:
        entries = entries * level_of(key, extent, split, -0.22, 0.18)
    return jnp.clip(entries, -bound, bound).astype(kind)


def setup_inputs(seed: int = 0) -> dict:
    key_of = jax.random.split(jax.random.key(seed), 8)
    multipoles = centred(key_of[0], (LEAVES, Q), 1.0, 6.0, ((0, 256),))
    translations = centred(key_of[1], (NT, Q, Q), (Q * NL) ** -0.5, 0.09375)
    send_index = plant(jax.random.randint(key_of[2], (DEVICES, DEVICES, CAP), 0, LEAF_DEV), jax.random.fold_in(key_of[2], 1), 0, LEAF_DEV - 1).astype(jnp.int32)
    far_slots = plant(jax.random.randint(key_of[3], (LEAVES, NL), 0, SLOTS), jax.random.fold_in(key_of[3], 1), 0, SLOTS - 1).astype(jnp.int32)
    far_types = plant(jax.random.randint(key_of[4], (LEAVES, NL), 0, NT), jax.random.fold_in(key_of[4], 1), 0, NT - 1).astype(jnp.int32)
    near_list = plant(jax.random.randint(key_of[5], (LEAVES, NN), 0, LEAF_DEV + 2 * HALO), jax.random.fold_in(key_of[5], 1), 0, (LEAF_DEV + 2 * HALO) - 1).astype(jnp.int32)
    particles = centred(key_of[6], (LEAVES, 6, P_SIZE), 1.0, 4.0, ((0, 256),), jnp.float32)
    return {"multipoles": multipoles, "translations": translations, "send_index": send_index, "far_slots": far_slots, "far_types": far_types, "near_list": near_list, "particles": particles}


EPS2 = 0.25
BLOCK = 8


def stokes_block(targets, sources):
    forces = sources[:, :, 3:6]
    d0 = targets[:, None, 0, :, None] - sources[:, :, 0, None, :]
    d1 = targets[:, None, 1, :, None] - sources[:, :, 1, None, :]
    d2 = targets[:, None, 2, :, None] - sources[:, :, 2, None, :]
    f0 = forces[:, :, 0, None, :]
    f1 = forces[:, :, 1, None, :]
    f2 = forces[:, :, 2, None, :]
    dist2 = d0 * d0 + d1 * d1 + d2 * d2
    inner = d0 * f0 + d1 * f1 + d2 * f2
    weight = (dist2 + EPS2) ** -1.5
    near = dist2 + 2.0 * EPS2
    scale = 1.0 / (8.0 * jnp.pi)
    u0 = jnp.sum((f0 * near + d0 * inner) * weight, axis=(1, 3))
    u1 = jnp.sum((f1 * near + d1 * inner) * weight, axis=(1, 3))
    u2 = jnp.sum((f2 * near + d2 * inner) * weight, axis=(1, 3))
    return jnp.stack([u0, u1, u2], axis=1) * scale


def reference(multipoles, translations, send_index, far_slots, far_types, near_list, particles):
    zeros = jnp.zeros((HALO, 6, P_SIZE), jnp.float32)
    padded = jnp.concatenate([zeros, particles, zeros], axis=0)
    kernels = translations.astype(jnp.float32)

    def one_device(rank):
        start = rank * LEAF_DEV
        slots = lax.dynamic_slice_in_dim(far_slots, start, LEAF_DEV, 0)
        types = lax.dynamic_slice_in_dim(far_types, start, LEAF_DEV, 0)
        source = slots // CAP
        column = slots % CAP
        leaf = send_index[source, rank, column]
        rows = multipoles[source * LEAF_DEV + leaf].astype(jnp.float32)
        onehot = (types[:, :, None] == jnp.arange(NT, dtype=jnp.int32)[None, None, :]).astype(jnp.float32)
        summed = jnp.einsum("lnt,lnq->ltq", onehot, rows)
        summed = lax.optimization_barrier(summed.astype(jnp.bfloat16)).astype(jnp.float32)
        expansion = jnp.einsum("ltq,tqp->lp", summed, kernels)
        mine = lax.dynamic_slice_in_dim(particles, start, LEAF_DEV, 0)
        neighbours = lax.dynamic_slice_in_dim(near_list, start, LEAF_DEV, 0) + start
        mine = mine.reshape(LEAF_DEV // BLOCK, BLOCK, 6, P_SIZE)
        neighbours = neighbours.reshape(LEAF_DEV // BLOCK, BLOCK, NN)

        def per_block(pair):
            targets, index = pair
            return stokes_block(targets, padded[index])

        speeds = lax.map(per_block, (mine, neighbours)).reshape(LEAF_DEV, 3, P_SIZE)
        return expansion, speeds

    expansions, speeds = lax.map(one_device, jnp.arange(DEVICES, dtype=jnp.int32))
    return expansions.reshape(LEAVES, Q), speeds.reshape(LEAVES, 3, P_SIZE)
```

```python
import functools
import math

import jax
import jax.numpy as jnp
from jax import lax
from jax.experimental import pallas as pl
from jax.experimental.pallas import tpu as pltpu
from jax.sharding import PartitionSpec as P

Q = 256
P_SIZE = 128
NT = 16
NN = 8
CAP = 2
HALO = 16
EPS2 = 0.25
NLF = 256
NE = NLF + 2 * HALO
UNROLL = 4
bf = jnp.bfloat16
f32 = jnp.float32


def split3(v):
    a=v.astype(bf).astype(f32); r=v-a
    b=r.astype(bf).astype(f32)
    return a,b,r-b

def near_kernel(near_ref, before_ref, mine_ref, after_ref, out_ref, ext, tgt, bt, gb, wa, wb, acc, *, U):
    rows=lax.broadcasted_iota(jnp.int32,(8,128),0)
    lane=lax.broadcasted_iota(jnp.int32,(1,128),1)
    z8=jnp.zeros((8,128),f32)
    ext[0:8,:]=z8
    ext[(NE+1)*8:(NE+2)*8,:]=z8
    def cp(ref,base,n):
        def one(e,_):
            r0=pl.multiple_of((base+e+1)*8,8)
            ext[pl.ds(r0,8),:]=z8
            ext[pl.ds(r0,6),:]=ref[e]
            return 0
        lax.fori_loop(0,n,one,0,unroll=8)
    cp(before_ref,0,16); cp(mine_ref,16,256); cp(after_ref,272,16)
    def bc(r): return jnp.broadcast_to(ext[pl.ds(r,1),:],(8,128))
    lo3=rows<3; lo6=rows<6; is6=rows==6
    def one(e):
        r0=(e+1)*8
        y=[bc(r0+c) for c in range(3)]; f=[bc(r0+3+c) for c in range(3)]
        Pt=ext[pl.ds(r0,8),:]; Pm=ext[pl.ds(r0+3,8),:]; Pq=ext[pl.ds(r0-3,8),:]
        n=y[0]*y[0]+y[1]*y[1]+y[2]*y[2]
        a=y[0]*f[0]+y[1]*f[1]+y[2]*f[2]
        t0=jnp.where(lo3,n*Pm+a*Pt,jnp.where(lo6,Pt,jnp.where(is6,a,y[2]*f[2])))
        t1=jnp.where(lo3,y[0]*Pm,jnp.where(lo6,y[1]*Pt,y[2]*Pq))
        t=jnp.concatenate([t0,t1],axis=0)
        g1,g2,g3=split3(t)
        gb[e]=jnp.concatenate([g1,g2,g3],axis=0).astype(bf)
        Q=jnp.where(lo3,Pt,Pq)
        q1,q2,q3=split3(Q)
        m=split3(n+EPS2)
        M=[jnp.where(is6,v,1.0) for v in m]
        src=jnp.concatenate([jnp.where(lo6,q1,M[0]),jnp.where(lo3,q1,jnp.where(lo6,q2,M[1])),jnp.where(lo3,q2,jnp.where(lo6,q3,M[2])),z8],axis=0)
        nn=split3(n)
        Nn=[jnp.where(is6,1.0,v) for v in nn]
        d1,d2,d3=-2.0*q1,-2.0*q2,-2.0*q3
        tg=jnp.concatenate([jnp.where(lo3,d1,jnp.where(lo6,d2,Nn[0])),jnp.where(lo3,d3,jnp.where(lo6,d1,Nn[1])),jnp.where(lo3,d2,jnp.where(lo6,d1,Nn[2])),z8],axis=0)
        tgt[e]=tg.astype(bf)
        return src
    def four(i,_):
        s=jnp.concatenate([one(i*4+v) for v in range(4)],axis=0)
        B=s.T.astype(bf)
        for v in range(4):
            bt[i*4+v]=jnp.where((lane>=32*v)&(lane<32*v+32),B,jnp.zeros((),bf))
        return 0
    lax.fori_loop(0,NE//4,four,0)
    Z=jnp.zeros((128,128),bf)
    def stage1(l,w,u):
        A=tgt[l+16]
        A4=jnp.concatenate([A,A,A,A],axis=0)
        R=jnp.concatenate([jnp.concatenate([A4,Z],axis=1),jnp.concatenate([Z,A4],axis=1)],axis=0)
        for p in range(NN//2):
            k1=near_ref[2*p,l]; k2=near_ref[2*p+1,l]
            L=jnp.concatenate([bt[k1],bt[k2]],axis=1)
            s=jnp.dot(L,R,preferred_element_type=f32)
            v=lax.rsqrt(s)
            w3=(v*v*v).astype(bf)
            w[u,p*256:p*256+128,:]=w3[:,:128]
            w[u,p*256+128:p*256+256,:]=w3[:,128:]
    def stage2(l,w,u):
        G=jnp.concatenate([gb[near_ref[k,l]] for k in range(NN)],axis=1)
        T=jnp.dot(G,w[u],preferred_element_type=f32)
        acc[pl.ds(pl.multiple_of(l*16,16),16),:]=T[0:16]+T[16:32]+T[32:48]
    for u in range(U): stage1(u,wa,u)
    def it(i,_):
        b=i*2*U
        for u in range(U):
            stage1(b+U+u,wb,u)
            stage2(b+u,wa,u)
        for u in range(U):
            stage1(jnp.minimum(b+2*U+u,NLF-1),wa,u)
            stage2(b+U+u,wb,u)
        return 0
    lax.fori_loop(0,NLF//(2*U),it,0)
    scale=1.0/(8.0*math.pi)
    def fin(g,_):
        x=[mine_ref[pl.ds(g*8,8),c,:] for c in range(3)]
        t=[acc[pl.ds(g*8*16+r,8,stride=16),:] for r in range(16)]
        n=x[0]*x[0]+x[1]*x[1]+x[2]*x[2]+2*EPS2
        N=t[0:3]; F=t[3:6]; A=t[6]
        Ym=[t[8:11],t[11:14],[t[14],t[15],t[7]]]
        xf=x[0]*F[0]+x[1]*F[1]+x[2]*F[2]-A
        for c in range(3):
            v=n*F[c]+N[c]+x[c]*xf
            for b in range(3):
                v=v-x[b]*(2.0*Ym[b][c]+Ym[c][b])
            out_ref[c,pl.ds(g*8,8),:]=v*scale
        return 0
    lax.fori_loop(0,32,fin,0)


def near(near_list, before, mine, after):
    return pl.pallas_call(
        functools.partial(near_kernel, U=UNROLL),
        out_shape=jax.ShapeDtypeStruct((3, NLF, P_SIZE), f32),
        in_specs=[pl.BlockSpec(memory_space=pltpu.SMEM)] + [pl.BlockSpec(memory_space=pltpu.VMEM)] * 3,
        out_specs=pl.BlockSpec(memory_space=pltpu.VMEM),
        scratch_shapes=[
            pltpu.VMEM(((NE + 2) * 8, 128), f32),
            pltpu.VMEM((NE, 32, 128), bf),
            pltpu.VMEM((NE, 128, 128), bf),
            pltpu.VMEM((NE, 48, 128), bf),
            pltpu.VMEM((UNROLL, 1024, 128), bf),
            pltpu.VMEM((UNROLL, 1024, 128), bf),
            pltpu.VMEM((NLF * 16, 128), f32),
        ],
        compiler_params=pltpu.CompilerParams(vmem_limit_bytes=48 * 2**20),
        cost_estimate=pl.CostEstimate(flops=60 * 10**9, bytes_accessed=2 * 10**6, transcendentals=33 * 10**6),
    )(near_list.T, before, mine, after)


def halo(x, axes):
    devices = lax.axis_size(axes)
    up = [(i, i + 1) for i in range(devices - 1)]
    down = [(j, i) for i, j in up]
    before = lax.ppermute(x[x.shape[0] - HALO :], axes, up)
    after = lax.ppermute(x[:HALO], axes, down)
    return before, after


def body(multipoles, translations, send_index, far_slots, far_types, near_list, particles):
    depth = lax.axis_size("gz")
    devices_all = send_index.shape[1]
    planes = devices_all // depth
    before, after = halo(particles, ("gx", "gy", "gz"))
    outgoing = multipoles[send_index[0]]
    outgoing = outgoing.reshape(planes, depth, CAP, Q)
    incoming = lax.all_to_all(
        lax.all_to_all(outgoing, ("gx", "gy"), split_axis=0, concat_axis=0, tiled=True),
        "gz",
        split_axis=1,
        concat_axis=1,
        tiled=True,
    )
    incoming = incoming.reshape(devices_all * CAP, Q)
    rows = incoming[far_slots]
    onehot = (far_types[:, :, None] == jnp.arange(NT, dtype=jnp.int32)[None, None, :]).astype(bf)
    summed = jnp.einsum("lnt,lnq->ltq", onehot, rows, preferred_element_type=f32).astype(bf)
    expansion = jnp.einsum("ltq,tqp->lp", summed, translations, preferred_element_type=f32)
    speeds = near(near_list, before, particles, after)
    return (expansion, jnp.transpose(speeds, (1, 0, 2)))


def solution(mesh):
    placed = (
        P(("gx", "gy", "gz"), None),
        P(),
        P(("gx", "gy", "gz"), None, None),
        P(("gx", "gy", "gz"), None),
        P(("gx", "gy", "gz"), None),
        P(("gx", "gy", "gz"), None),
        P(("gx", "gy", "gz"), None, None),
    )
    return jax.shard_map(
        body,
        mesh=mesh,
        in_specs=placed,
        out_specs=(P(("gx", "gy", "gz"), None), P(("gx", "gy", "gz"), None, None)),
        check_vma=False,
    )
```

```python
import functools
import math

import jax
import jax.numpy as jnp
from jax import lax
from jax.experimental import pallas as pl
from jax.experimental.pallas import tpu as pltpu
from jax.sharding import PartitionSpec as P

Q = 256
P_SIZE = 128
NT = 16
NL = 16
NN = 8
CAP = 2
HALO = 16
EPS2 = 0.25
NLF = 256
NE = NLF + 2 * HALO
UNROLL = 4
bf = jnp.bfloat16
f32 = jnp.float32


def split3(v):
    a=v.astype(bf).astype(f32); r=v-a
    b=r.astype(bf).astype(f32)
    return a,b,r-b

def near_kernel(near_ref, before_ref, mine_ref, after_ref, out_ref, tgt, bt, gb, wa, wb, acc, *, U, PU):
    rows=lax.broadcasted_iota(jnp.int32,(8,128),0)
    lane=lax.broadcasted_iota(jnp.int32,(1,128),1)
    z8=jnp.zeros((8,128),f32)
    lo3=rows<3; lo6=rows<6; is6=rows==6
    is0=(rows==0)|(rows==3); is1=(rows==1)|(rows==4)
    keep=[((lane>=32*v)&(lane<32*v+32)).astype(f32).astype(bf) for v in range(4)]
    def one(ref,e,eg):
        y=[jnp.broadcast_to(ref[c,pl.ds(e,1),:],(8,128)) for c in range(6)]
        y,f=y[:3],y[3:]
        n=y[0]*y[0]+y[1]*y[1]+y[2]*y[2]
        a=y[0]*f[0]+y[1]*f[1]+y[2]*f[2]
        Q=jnp.where(is0,y[0],jnp.where(is1,y[1],y[2]))
        F=jnp.where(is0,f[0],jnp.where(is1,f[1],f[2]))
        t0=jnp.where(lo3,n*F+a*Q,jnp.where(lo6,F,jnp.where(is6,a,y[2]*f[2])))
        t1=jnp.where(lo3,y[0],jnp.where(lo6,y[1],y[2]))*jnp.where(lo6,F,jnp.where(is6,f[0],f[1]))
        t=jnp.concatenate([t0,t1],axis=0)
        g1=t.astype(bf)
        g2=(t-g1.astype(f32)).astype(bf)
        gb[eg]=jnp.concatenate([g1,g2],axis=0)
        q1,q2,q3=split3(Q)
        m=split3(n+EPS2)
        M=[jnp.where(is6,v,1.0) for v in m]
        src=jnp.concatenate([jnp.where(lo6,q1,M[0]),jnp.where(lo3,q1,jnp.where(lo6,q2,M[1])),jnp.where(lo3,q2,jnp.where(lo6,q3,M[2])),z8],axis=0)
        if ref is mine_ref:
            nn=split3(n)
            Nn=[jnp.where(is6,1.0,v) for v in nn]
            d1,d2,d3=-2.0*q1,-2.0*q2,-2.0*q3
            tg=jnp.concatenate([jnp.where(lo3,d1,jnp.where(lo6,d2,Nn[0])),jnp.where(lo3,d3,jnp.where(lo6,d1,Nn[1])),jnp.where(lo3,d2,jnp.where(lo6,d1,Nn[2])),z8],axis=0)
            tgt[e]=tg.astype(bf)
        return src.astype(bf)
    def prep(ref,base,n,un):
        def four(i,_):
            for w in range(un):
                o=(i*un+w)*4
                B=jnp.concatenate([one(ref,o+v,base+o+v) for v in range(4)],axis=0).T
                for v in range(4):
                    bt[base+o+v]=B*keep[v]
            return 0
        lax.fori_loop(0,n//(4*un),four,0)
    prep(before_ref,0,16,2); prep(mine_ref,16,256,PU); prep(after_ref,272,16,2)
    Z=jnp.zeros((128,128),bf)
    def stage1(l,w,u):
        A=tgt[l]
        A4=jnp.concatenate([A,A,A,A],axis=0)
        R=jnp.concatenate([jnp.concatenate([A4,Z],axis=1),jnp.concatenate([Z,A4],axis=1)],axis=0)
        D=[]
        for p in range(NN//2):
            k1=near_ref[2*p,l]; k2=near_ref[2*p+1,l]
            D.append(jnp.concatenate([bt[k1],bt[k2]],axis=1))
        s=jnp.dot(jnp.concatenate(D,axis=0),R,preferred_element_type=f32)
        v=lax.rsqrt(s)
        w3=(v*v*v).astype(bf)
        for p in range(NN//2):
            w[u,p*256:p*256+128,:]=w3[p*128:p*128+128,:128]
            w[u,p*256+128:p*256+256,:]=w3[p*128:p*128+128,128:]
    def stage2(l,w,u):
        G=jnp.concatenate([gb[near_ref[k,l]] for k in range(NN)],axis=1)
        T=jnp.dot(G,w[u],preferred_element_type=f32)
        acc[pl.ds(pl.multiple_of(l*16,16),16),:]=T[0:16]+T[16:32]
    for u in range(U): stage1(u,wa,u)
    def it(i,_):
        b=i*2*U
        for u in range(U):
            stage1(b+U+u,wb,u)
            stage2(b+u,wa,u)
        for u in range(U):
            stage1(jnp.minimum(b+2*U+u,NLF-1),wa,u)
            stage2(b+U+u,wb,u)
        return 0
    lax.fori_loop(0,NLF//(2*U),it,0)
    scale=1.0/(8.0*math.pi)
    def fin(g,_):
        x=[mine_ref[c,pl.ds(g*8,8),:] for c in range(3)]
        t=[acc[pl.ds(g*8*16+r,8,stride=16),:] for r in range(16)]
        n=x[0]*x[0]+x[1]*x[1]+x[2]*x[2]+2*EPS2
        N=t[0:3]; F=t[3:6]; A=t[6]
        Ym=[t[8:11],t[11:14],[t[14],t[15],t[7]]]
        xf=x[0]*F[0]+x[1]*F[1]+x[2]*F[2]-A
        for c in range(3):
            v=n*F[c]+N[c]+x[c]*xf
            for b in range(3):
                v=v-x[b]*(2.0*Ym[b][c]+Ym[c][b])
            out_ref[c,pl.ds(g*8,8),:]=v*scale
        return 0
    lax.fori_loop(0,32,fin,0)

def near(near_list, before, mine, after):
    return pl.pallas_call(
        functools.partial(near_kernel, U=UNROLL, PU=4),
        out_shape=jax.ShapeDtypeStruct((3, NLF, P_SIZE), f32),
        in_specs=[pl.BlockSpec(memory_space=pltpu.SMEM)] + [pl.BlockSpec(memory_space=pltpu.VMEM)] * 3,
        out_specs=pl.BlockSpec(memory_space=pltpu.VMEM),
        scratch_shapes=[
            pltpu.VMEM((NLF, 32, 128), bf),
            pltpu.VMEM((NE, 128, 128), bf),
            pltpu.VMEM((NE, 32, 128), bf),
            pltpu.VMEM((UNROLL, 1024, 128), bf),
            pltpu.VMEM((UNROLL, 1024, 128), bf),
            pltpu.VMEM((NLF * 16, 128), f32),
        ],
        compiler_params=pltpu.CompilerParams(vmem_limit_bytes=48 * 2**20),
        cost_estimate=pl.CostEstimate(flops=60 * 10**9, bytes_accessed=2 * 10**6, transcendentals=33 * 10**6),
    )(near_list.T, before, mine, after)


def far_kernel(enc_ref, r_ref, t_ref, out_ref, g_ref):
    sub = lax.broadcasted_iota(jnp.int32, (256, 256), 0)
    leaf = lax.broadcasted_iota(jnp.int32, (1, 256), 1) // NL
    lane = lax.broadcasted_iota(jnp.int32, (1, 512), 1).astype(f32)
    def block(b, _):
        e = enc_ref[pl.ds(b, 1), :]
        slot = (e & 511).astype(f32)
        cls = (e >> 9) * 16 + leaf
        col = jnp.concatenate([jnp.broadcast_to(slot[:, h * 128 : h * 128 + 128], (128, 128)).T for h in range(2)], axis=0)
        col = jnp.concatenate([col] * 4, axis=1)
        pick = (col == lane).astype(f32).astype(bf)
        rows = jnp.dot(pick, r_ref[...], preferred_element_type=f32).astype(bf)
        own = (sub == cls).astype(f32).astype(bf)
        g = jnp.dot(own, rows, preferred_element_type=f32).astype(bf)
        for t in range(NT):
            g_ref[t, pl.ds(pl.multiple_of(b * 16, 16), 16), :] = g[t * 16 : t * 16 + 16]
        return 0
    lax.fori_loop(0, 16, block, 0, unroll=2)
    acc = jnp.dot(g_ref[0], t_ref[0], preferred_element_type=f32)
    for t in range(1, NT):
        acc = acc + jnp.dot(g_ref[t], t_ref[t], preferred_element_type=f32)
    out_ref[...] = acc


def far(enc, received, translations):
    return pl.pallas_call(far_kernel, out_shape=jax.ShapeDtypeStruct((256,Q),f32),
        in_specs=[pl.BlockSpec(memory_space=pltpu.VMEM)]*3, out_specs=pl.BlockSpec(memory_space=pltpu.VMEM),
        scratch_shapes=[pltpu.VMEM((NT,256,Q),bf)],
        compiler_params=pltpu.CompilerParams(vmem_limit_bytes=24*2**20))(enc,received,translations)


def halo(x, axes):
    devices = lax.axis_size(axes)
    odd = lax.axis_index(axes) % 2 == 1
    leading, last = x[:, :HALO], x[:, x.shape[1] - HALO :]
    first = [(i, i ^ 1) for i in range(devices)]
    second = [(i, i + 1) for i in range(1, devices - 1, 2)]
    second += [(j, i) for i, j in second]
    one = lax.ppermute(jnp.where(odd, leading, last), axes, first)
    two = lax.ppermute(jnp.where(odd, last, leading), axes, second)
    return jnp.where(odd, one, two), jnp.where(odd, two, one)


def body(multipoles, translations, send_index, far_slots, far_types, near_list, particles):
    axes = ("gx", "gy", "gz")
    devices = send_index.shape[1]
    mine = jnp.transpose(particles, (1, 0, 2))
    before, after = halo(mine, axes)
    outgoing = multipoles[send_index[0]].reshape(devices, CAP * Q // 128, 128)
    incoming = lax.all_to_all(outgoing, axes, split_axis=0, concat_axis=0, tiled=True)
    entries = (far_slots + devices * CAP * far_types).reshape(16, NLF * NL // 16)
    speeds = near(near_list, before, mine, after)
    expansion = far(entries, incoming.reshape(devices * CAP, Q), translations)
    return (expansion, jnp.transpose(speeds, (1, 0, 2)))


def solution(mesh):
    placed = (
        P(("gx", "gy", "gz"), None),
        P(),
        P(("gx", "gy", "gz"), None, None),
        P(("gx", "gy", "gz"), None),
        P(("gx", "gy", "gz"), None),
        P(("gx", "gy", "gz"), None),
        P(("gx", "gy", "gz"), None, None),
    )
    return jax.shard_map(
        body,
        mesh=mesh,
        in_specs=placed,
        out_specs=(P(("gx", "gy", "gz"), None), P(("gx", "gy", "gz"), None, None)),
        check_vma=False,
    )
```

```python
import functools
import math

import jax
import jax.numpy as jnp
from jax import lax
from jax.experimental import pallas as pl
from jax.experimental.pallas import tpu as pltpu
from jax.sharding import PartitionSpec as P

Q = 256
P_SIZE = 128
NT = 16
NL = 16
NN = 8
CAP = 2
HALO = 16
EPS2 = 0.25
NLF = 256
NE = NLF + 2 * HALO
UNROLL = 4
BLOCKS = 8
bf = jnp.bfloat16
f32 = jnp.float32


def split3(v):
    a=v.astype(bf).astype(f32); r=v-a
    b=r.astype(bf).astype(f32)
    return a,b,r-b

def near_kernel(near_hbm, before_ref, mine_hbm, after_ref, out_ref, tgt, bt, gb, wa, wb, acc, mine_ref, near_ref, sems, *, U, PU):
    copies=[pltpu.make_async_copy(mine_hbm,mine_ref,sems.at[0]),pltpu.make_async_copy(near_hbm,near_ref,sems.at[1])]
    for copy in copies: copy.start()
    rows=lax.broadcasted_iota(jnp.int32,(8,128),0)
    lane=lax.broadcasted_iota(jnp.int32,(1,128),1)
    z8=jnp.zeros((8,128),f32)
    lo3=rows<3; lo6=rows<6; is6=rows==6
    is0=(rows==0)|(rows==3); is1=(rows==1)|(rows==4)
    keep=[((lane>=32*v)&(lane<32*v+32)).astype(f32).astype(bf) for v in range(4)]
    is7=rows==7; end=lo3|is7
    scale_t=jnp.where(lo6,-2.0,jnp.where(is6,0.0,1.0)); fixed_t=jnp.where(is6,1.0,0.0)
    def one(ref,e,eg):
        y=[jnp.broadcast_to(ref[c,pl.ds(e,1),:],(8,128)) for c in range(6)]
        y,f=y[:3],y[3:]
        n=y[0]*y[0]+y[1]*y[1]+y[2]*y[2]
        a=y[0]*f[0]+y[1]*f[1]+y[2]*f[2]
        Q=jnp.where(is0,y[0],jnp.where(is1,y[1],y[2]))
        F=jnp.where(is0,f[0],jnp.where(is1,f[1],f[2]))
        t0=jnp.where(lo3,n*F+a*Q,jnp.where(lo6,F,jnp.where(is6,a,y[2]*f[2])))
        t1=jnp.where(lo3,y[0],jnp.where(lo6,y[1],y[2]))*jnp.where(lo6,F,jnp.where(is6,f[0],f[1]))
        t=jnp.concatenate([t0,t1],axis=0)
        g1=t.astype(bf)
        g2=(t-g1.astype(f32)).astype(bf)
        gb[eg]=jnp.concatenate([g1,g2],axis=0)
        q1,q2,q3=split3(jnp.where(lo6,Q,jnp.where(is6,n+EPS2,n)))
        src=jnp.concatenate([jnp.where(is7,1.0,q1),jnp.where(is7,1.0,jnp.where(lo3,q1,q2)),jnp.where(is7,1.0,jnp.where(lo3,q2,q3)),z8],axis=0)
        if ref is mine_ref:
            tg=[jnp.where(end,q1,q2),jnp.where(lo3,q3,jnp.where(is7,q2,q1)),jnp.where(lo3,q2,jnp.where(is7,q3,q1))]
            tgt[e]=jnp.concatenate([v*scale_t+fixed_t for v in tg]+[z8],axis=0).astype(bf)
        return src.astype(bf)
    def prep(ref,base,n,un):
        def four(i,_):
            for w in range(un):
                o=(i*un+w)*4
                B=jnp.concatenate([one(ref,o+v,base+o+v) for v in range(4)],axis=0).T
                for v in range(4):
                    bt[base+o+v]=B*keep[v]
            return 0
        lax.fori_loop(0,n//(4*un),four,0)
    prep(before_ref,0,16,4); prep(after_ref,272,16,4)
    for copy in copies: copy.wait()
    prep(mine_ref,16,256,PU)
    Z=jnp.zeros((128,128),bf)
    def stage1(l,w,u):
        A=tgt[l]
        A4=jnp.concatenate([A,A,A,A],axis=0)
        R=jnp.concatenate([jnp.concatenate([A4,Z],axis=1),jnp.concatenate([Z,A4],axis=1)],axis=0)
        D=[]
        for p in range(NN//2):
            k1=near_ref[2*p,l]; k2=near_ref[2*p+1,l]
            D.append(jnp.concatenate([bt[k1],bt[k2]],axis=1))
        s=jnp.dot(jnp.concatenate(D,axis=0),R,preferred_element_type=f32)
        v=lax.rsqrt(s)
        w3=(v*v*v).astype(bf)
        for p in range(NN//2):
            w[u,p*256:p*256+128,:]=w3[p*128:p*128+128,:128]
            w[u,p*256+128:p*256+256,:]=w3[p*128:p*128+128,128:]
    def stage2(l,w,u):
        G=jnp.concatenate([gb[near_ref[k,l]] for k in range(NN)],axis=1)
        T=jnp.dot(G,w[u],preferred_element_type=f32)
        acc[pl.ds(pl.multiple_of(l*16,16),16),:]=T[0:16]+T[16:32]
    for u in range(U): stage1(u,wa,u)
    scale=1.0/(8.0*math.pi)
    def fin(g,_):
        x=[mine_ref[c,pl.ds(g*8,8),:] for c in range(3)]
        t=[acc[pl.ds(g*8*16+r,8,stride=16),:] for r in range(16)]
        n=x[0]*x[0]+x[1]*x[1]+x[2]*x[2]+2*EPS2
        N=t[0:3]; F=t[3:6]; A=t[6]
        Ym=[t[8:11],t[11:14],[t[14],t[15],t[7]]]
        xf=x[0]*F[0]+x[1]*F[1]+x[2]*F[2]-A
        for c in range(3):
            v=n*F[c]+N[c]+x[c]*xf
            for b in range(3):
                v=v-x[b]*(2.0*Ym[b][c]+Ym[c][b])
            out_ref[c,pl.ds(g*8,8),:]=v*scale
        return 0
    def it(i,_):
        b=i*2*U
        fin(jnp.maximum(i-1,0),0)
        for u in range(U):
            stage1(b+U+u,wb,u)
            stage2(b+u,wa,u)
        for u in range(U):
            stage1(jnp.minimum(b+2*U+u,NLF-1),wa,u)
            stage2(b+U+u,wb,u)
        return 0
    lax.fori_loop(0,NLF//(2*U),it,0)
    fin(NLF//8-1,0)

def near(near_list, before, mine, after):
    return pl.pallas_call(
        functools.partial(near_kernel, U=UNROLL, PU=4),
        out_shape=jax.ShapeDtypeStruct((3, NLF, P_SIZE), f32),
        in_specs=[pl.BlockSpec(memory_space=m) for m in (pltpu.HBM, pltpu.VMEM, pltpu.HBM, pltpu.VMEM)],
        out_specs=pl.BlockSpec(memory_space=pltpu.VMEM),
        scratch_shapes=[
            pltpu.VMEM((NLF, 32, 128), bf),
            pltpu.VMEM((NE, 128, 128), bf),
            pltpu.VMEM((NE, 32, 128), bf),
            pltpu.VMEM((UNROLL, 1024, 128), bf),
            pltpu.VMEM((UNROLL, 1024, 128), bf),
            pltpu.VMEM((NLF * 16, 128), f32),
            pltpu.VMEM((6, NLF, 128), f32),
            pltpu.SMEM((NN, NLF), jnp.int32),
            pltpu.SemaphoreType.DMA((2,)),
        ],
        compiler_params=pltpu.CompilerParams(vmem_limit_bytes=32 * 2**20),
        cost_estimate=pl.CostEstimate(flops=60 * 10**9, bytes_accessed=2 * 10**6, transcendentals=33 * 10**6),
    )(near_list.T, before, mine, after)


def far_kernel(enc_ref, r_ref, t_ref, out_ref, g_ref, s_ref):
    s_ref[...] = r_ref[...].reshape(1024, 128).astype(f32)
    table = jnp.concatenate([s_ref[pl.ds(h, 512, stride=2), :] for h in range(2)], axis=1).astype(bf)
    sub = lax.broadcasted_iota(jnp.int32, (256, 256), 0)
    leaf = lax.broadcasted_iota(jnp.int32, (1, 256), 1) // NL
    lane = lax.broadcasted_iota(jnp.int32, (1, 512), 1).astype(f32)
    def picks(b):
        e = enc_ref[pl.ds(b, 1), :]
        slot = (e & 511).astype(f32)
        cls = (e >> 9) * 16 + leaf
        col = jnp.concatenate([jnp.broadcast_to(slot[:, h * 128 : h * 128 + 128], (128, 128)).T for h in range(2)], axis=0)
        col = jnp.concatenate([col] * 4, axis=1)
        pick = (col == lane).astype(f32).astype(bf)
        own = (sub == cls).astype(f32).astype(bf)
        return pick, own
    def block(i, _):
        both = [picks(i * BLOCKS + j) for j in range(BLOCKS)]
        rows = jnp.dot(jnp.concatenate([p for p, _ in both], axis=0), table, preferred_element_type=f32).astype(bf)
        for j in range(BLOCKS):
            g = jnp.dot(both[j][1], rows[j * 256 : j * 256 + 256], preferred_element_type=f32).astype(bf)
            b = pl.multiple_of((i * BLOCKS + j) * 16, 16)
            for t in range(NT):
                g_ref[pl.ds(b, 16), t * Q : t * Q + Q] = g[t * 16 : t * 16 + 16]
        return 0
    lax.fori_loop(0, 16 // BLOCKS, block, 0)
    out_ref[...] = jnp.dot(g_ref[...], t_ref[...].reshape(NT * Q, Q), preferred_element_type=f32)


def far(enc, received, translations):
    return pl.pallas_call(far_kernel, out_shape=jax.ShapeDtypeStruct((256,Q),f32),
        in_specs=[pl.BlockSpec(memory_space=pltpu.VMEM)]*3, out_specs=pl.BlockSpec(memory_space=pltpu.VMEM),
        scratch_shapes=[pltpu.VMEM((256,NT*Q),bf), pltpu.VMEM((1024,128),f32)],
        compiler_params=pltpu.CompilerParams(vmem_limit_bytes=24*2**20))(enc,received,translations)


def pick_kernel(i_ref, m_ref, out_ref, rows_ref):
    lane = lax.broadcasted_iota(jnp.int32, (1, 256), 1).astype(f32)
    for c in range(2):
        index = i_ref[c : c + 1, :].astype(f32)
        col = jnp.concatenate([jnp.broadcast_to(index[:, h * 128 : h * 128 + 128], (128, 128)).T for h in range(2)], axis=0)
        pick = (jnp.concatenate([col, col], axis=1) == lane).astype(f32).astype(bf)
        got = jnp.dot(pick, m_ref[...], preferred_element_type=f32)
        for h in range(2):
            rows_ref[pl.ds(2 * c + h, 256, stride=4), :] = got[:, h * 128 : h * 128 + 128]
    out_ref[...] = rows_ref[...].astype(bf).reshape(256, 4, 128)


def pick(index, m):
    return pl.pallas_call(
        pick_kernel,
        out_shape=jax.ShapeDtypeStruct((256, 4, 128), bf),
        in_specs=[pl.BlockSpec(memory_space=pltpu.VMEM)] * 2,
        out_specs=pl.BlockSpec(memory_space=pltpu.VMEM),
        scratch_shapes=[pltpu.VMEM((1024, 128), f32)],
        cost_estimate=pl.CostEstimate(flops=4 * 10**9, bytes_accessed=10**7, transcendentals=0),
    )(index, m)


def halo(x, axes):
    devices = lax.axis_size(axes)
    odd = lax.axis_index(axes) % 2 == 1
    leading, last = x[:, :HALO], x[:, x.shape[1] - HALO :]
    first = [(i, i ^ 1) for i in range(devices)]
    second = [(i, i + 1) for i in range(1, devices - 1, 2)]
    second += [(j, i) for i, j in second]
    one = lax.ppermute(jnp.where(odd, leading, last), axes, first)
    two = lax.ppermute(jnp.where(odd, last, leading), axes, second)
    return jnp.where(odd, one, two), jnp.where(odd, two, one)


def body(multipoles, translations, send_index, far_slots, far_types, near_list, particles):
    axes = ("gx", "gy", "gz")
    devices = send_index.shape[1]
    mine = jnp.transpose(particles, (1, 0, 2))
    before, after = halo(mine, axes)
    outgoing = pick(send_index[0].T, multipoles)
    incoming = lax.all_to_all(outgoing, axes, split_axis=0, concat_axis=0, tiled=True)
    entries = (far_slots + devices * CAP * far_types).reshape(16, NLF * NL // 16)
    speeds = near(near_list, before, mine, after)
    expansion = far(entries, incoming, translations)
    return (expansion, jnp.transpose(speeds, (1, 0, 2)))


def solution(mesh):
    placed = (
        P(("gx", "gy", "gz"), None),
        P(),
        P(("gx", "gy", "gz"), None, None),
        P(("gx", "gy", "gz"), None),
        P(("gx", "gy", "gz"), None),
        P(("gx", "gy", "gz"), None),
        P(("gx", "gy", "gz"), None, None),
    )
    return jax.shard_map(
        body,
        mesh=mesh,
        in_specs=placed,
        out_specs=(P(("gx", "gy", "gz"), None), P(("gx", "gy", "gz"), None, None)),
        check_vma=False,
    )
```

```python
import functools
import math

import jax
import jax.numpy as jnp
from jax import lax
from jax.experimental import pallas as pl
from jax.experimental.pallas import tpu as pltpu
from jax.sharding import PartitionSpec as P

Q = 256
P_SIZE = 128
NT = 16
NL = 16
NN = 8
CAP = 2
HALO = 16
EPS2 = 0.25
NLF = 256
NE = NLF + 2 * HALO
UNROLL = 16
BLOCKS = 8
bf = jnp.bfloat16
f32 = jnp.float32


def split3(v):
    a=v.astype(bf).astype(f32); r=v-a
    b=r.astype(bf).astype(f32)
    return a,b,r-b

def near_kernel(near_hbm, before_ref, mine_hbm, after_ref, out_ref, tgt, bt, gb, wa, wb, acc, mine_ref, near_ref, sems, *, U, PU):
    copies=[pltpu.make_async_copy(mine_hbm,mine_ref,sems.at[0]),pltpu.make_async_copy(near_hbm,near_ref,sems.at[1])]
    for copy in copies: copy.start()
    rows=lax.broadcasted_iota(jnp.int32,(8,128),0)
    lane=lax.broadcasted_iota(jnp.int32,(1,128),1)
    z8=jnp.zeros((8,128),f32)
    lo3=rows<3; lo6=rows<6; is6=rows==6
    is0=(rows==0)|(rows==3); is1=(rows==1)|(rows==4)
    keep=[((lane>=32*v)&(lane<32*v+32)).astype(f32).astype(bf) for v in range(4)]
    is7=rows==7; end=lo3|is7
    scale_t=jnp.where(lo6,-2.0,jnp.where(is6,0.0,1.0)); fixed_t=jnp.where(is6,1.0,0.0)
    def one(ref,e,eg):
        y=[jnp.broadcast_to(ref[c,pl.ds(e,1),:],(8,128)) for c in range(6)]
        y,f=y[:3],y[3:]
        n=y[0]*y[0]+y[1]*y[1]+y[2]*y[2]
        a=y[0]*f[0]+y[1]*f[1]+y[2]*f[2]
        Q=jnp.where(is0,y[0],jnp.where(is1,y[1],y[2]))
        F=jnp.where(is0,f[0],jnp.where(is1,f[1],f[2]))
        t0=jnp.where(lo3,n*F+a*Q,jnp.where(lo6,F,jnp.where(is6,a,y[2]*f[2])))
        t1=jnp.where(lo3,y[0],jnp.where(lo6,y[1],y[2]))*jnp.where(lo6,F,jnp.where(is6,f[0],f[1]))
        t=jnp.concatenate([t0,t1],axis=0)
        g1=t.astype(bf)
        g2=(t-g1.astype(f32)).astype(bf)
        gb[eg]=jnp.concatenate([g1,g2],axis=0)
        q1,q2,q3=split3(jnp.where(lo6,Q,jnp.where(is6,n+EPS2,n)))
        src=jnp.concatenate([jnp.where(is7,1.0,q1),jnp.where(is7,1.0,jnp.where(lo3,q1,q2)),jnp.where(is7,1.0,jnp.where(lo3,q2,q3)),z8],axis=0)
        if ref is mine_ref:
            tg=[jnp.where(end,q1,q2),jnp.where(lo3,q3,jnp.where(is7,q2,q1)),jnp.where(lo3,q2,jnp.where(is7,q3,q1))]
            tgt[e]=jnp.concatenate([v*scale_t+fixed_t for v in tg]+[z8],axis=0).astype(bf)
        return src.astype(bf)
    def prep(ref,base,n,un):
        def four(i,_):
            for w in range(un):
                o=(i*un+w)*4
                B=jnp.concatenate([one(ref,o+v,base+o+v) for v in range(4)],axis=0).T
                for v in range(4):
                    bt[base+o+v]=B*keep[v]
            return 0
        lax.fori_loop(0,n//(4*un),four,0)
    prep(before_ref,0,16,4); prep(after_ref,272,16,4)
    for copy in copies: copy.wait()
    prep(mine_ref,16,256,PU)
    Z=jnp.zeros((128,128),bf)
    def stage1(l,w,u):
        A4,B4=[jnp.concatenate([tgt[l+j]]*4,axis=0) for j in range(2)]
        R=jnp.concatenate([jnp.concatenate([A4,Z],axis=1),jnp.concatenate([Z,B4],axis=1)],axis=0)
        D=[jnp.concatenate([bt[near_ref[k,l+j]] for j in range(2)],axis=1) for k in range(NN)]
        s=jnp.dot(jnp.concatenate(D,axis=0),R,preferred_element_type=f32)
        v=lax.rsqrt(s)
        w3=(v*v*v).astype(bf)
        for j in range(2):
            w[u+j]=w3[:,j*128:j*128+128]
    def stage2(l,w,u):
        G=jnp.concatenate([gb[near_ref[k,l]] for k in range(NN)],axis=1)
        T=jnp.dot(G,w[u],preferred_element_type=f32)
        acc[pl.ds(pl.multiple_of(l*16,16),16),:]=T[0:16]+T[16:32]
    for u in range(0,U,2): stage1(u,wa,u)
    scale=1.0/(8.0*math.pi)
    def fin(g,_):
        x=[mine_ref[c,pl.ds(g*8,8),:] for c in range(3)]
        t=[acc[pl.ds(g*8*16+r,8,stride=16),:] for r in range(16)]
        n=x[0]*x[0]+x[1]*x[1]+x[2]*x[2]+2*EPS2
        N=t[0:3]; F=t[3:6]; A=t[6]
        Ym=[t[8:11],t[11:14],[t[14],t[15],t[7]]]
        xf=x[0]*F[0]+x[1]*F[1]+x[2]*F[2]-A
        for c in range(3):
            v=n*F[c]+N[c]+x[c]*xf
            for b in range(3):
                v=v-x[b]*(2.0*Ym[b][c]+Ym[c][b])
            out_ref[c,pl.ds(g*8,8),:]=v*scale
        return 0
    def it(i,_):
        b=i*2*U
        for j in range(2*U//8): fin(jnp.maximum(i-1,0)*(2*U//8)+j,0)
        for u in range(0,U,2):
            stage1(b+U+u,wb,u)
            stage2(b+u,wa,u)
            stage2(b+u+1,wa,u+1)
        for u in range(0,U,2):
            stage1(jnp.minimum(b+2*U+u,NLF-2),wa,u)
            stage2(b+U+u,wb,u)
            stage2(b+U+u+1,wb,u+1)
        return 0
    lax.fori_loop(0,NLF//(2*U),it,0)
    for j in range(2*U//8): fin(NLF//8-2*U//8+j,0)

def near(near_list, before, mine, after):
    return pl.pallas_call(
        functools.partial(near_kernel, U=UNROLL, PU=4),
        out_shape=jax.ShapeDtypeStruct((3, NLF, P_SIZE), f32),
        in_specs=[pl.BlockSpec(memory_space=m) for m in (pltpu.HBM, pltpu.VMEM, pltpu.HBM, pltpu.VMEM)],
        out_specs=pl.BlockSpec(memory_space=pltpu.VMEM),
        scratch_shapes=[
            pltpu.VMEM((NLF, 32, 128), bf),
            pltpu.VMEM((NE, 128, 128), bf),
            pltpu.VMEM((NE, 32, 128), bf),
            pltpu.VMEM((UNROLL, 1024, 128), bf),
            pltpu.VMEM((UNROLL, 1024, 128), bf),
            pltpu.VMEM((NLF * 16, 128), f32),
            pltpu.VMEM((6, NLF, 128), f32),
            pltpu.SMEM((NN, NLF), jnp.int32),
            pltpu.SemaphoreType.DMA((2,)),
        ],
        compiler_params=pltpu.CompilerParams(vmem_limit_bytes=32 * 2**20),
        cost_estimate=pl.CostEstimate(flops=60 * 10**9, bytes_accessed=2 * 10**6, transcendentals=33 * 10**6),
    )(near_list.T, before, mine, after)


def far_kernel(enc_ref, r_ref, t_ref, out_ref, g_ref, s_ref):
    s_ref[...] = r_ref[...].reshape(1024, 128).astype(f32)
    table = jnp.concatenate([s_ref[pl.ds(h, 512, stride=2), :] for h in range(2)], axis=1).astype(bf)
    sub = lax.broadcasted_iota(jnp.int32, (256, 256), 0)
    leaf = lax.broadcasted_iota(jnp.int32, (1, 256), 1) // NL
    lane = lax.broadcasted_iota(jnp.int32, (1, 512), 1).astype(f32)
    def picks(b):
        e = enc_ref[pl.ds(b, 1), :]
        slot = (e & 511).astype(f32)
        cls = (e >> 9) * 16 + leaf
        col = jnp.concatenate([jnp.broadcast_to(slot[:, h * 128 : h * 128 + 128], (128, 128)).T for h in range(2)], axis=0)
        col = jnp.concatenate([col] * 4, axis=1)
        pick = (col == lane).astype(f32).astype(bf)
        own = (sub == cls).astype(f32).astype(bf)
        return pick, own
    def block(i, _):
        both = [picks(i * BLOCKS + j) for j in range(BLOCKS)]
        rows = jnp.dot(jnp.concatenate([p for p, _ in both], axis=0), table, preferred_element_type=f32).astype(bf)
        for j in range(BLOCKS):
            g = jnp.dot(both[j][1], rows[j * 256 : j * 256 + 256], preferred_element_type=f32).astype(bf)
            b = pl.multiple_of((i * BLOCKS + j) * 16, 16)
            for t in range(NT):
                g_ref[pl.ds(b, 16), t * Q : t * Q + Q] = g[t * 16 : t * 16 + 16]
        return 0
    lax.fori_loop(0, 16 // BLOCKS, block, 0)
    out_ref[...] = jnp.dot(g_ref[...], t_ref[...].reshape(NT * Q, Q), preferred_element_type=f32)


def far(enc, received, translations):
    return pl.pallas_call(far_kernel, out_shape=jax.ShapeDtypeStruct((256,Q),f32),
        in_specs=[pl.BlockSpec(memory_space=pltpu.VMEM)]*3, out_specs=pl.BlockSpec(memory_space=pltpu.VMEM),
        scratch_shapes=[pltpu.VMEM((256,NT*Q),bf), pltpu.VMEM((1024,128),f32)],
        compiler_params=pltpu.CompilerParams(vmem_limit_bytes=24*2**20))(enc,received,translations)


def pick_kernel(i_ref, m_ref, out_ref, rows_ref):
    lane = lax.broadcasted_iota(jnp.int32, (1, 256), 1).astype(f32)
    for c in range(2):
        index = i_ref[c : c + 1, :].astype(f32)
        col = jnp.concatenate([jnp.broadcast_to(index[:, h * 128 : h * 128 + 128], (128, 128)).T for h in range(2)], axis=0)
        pick = (jnp.concatenate([col, col], axis=1) == lane).astype(f32).astype(bf)
        got = jnp.dot(pick, m_ref[...], preferred_element_type=f32)
        for h in range(2):
            rows_ref[pl.ds(2 * c + h, 256, stride=4), :] = got[:, h * 128 : h * 128 + 128]
    out_ref[...] = rows_ref[...].astype(bf).reshape(256, 4, 128)


def pick(index, m):
    return pl.pallas_call(
        pick_kernel,
        out_shape=jax.ShapeDtypeStruct((256, 4, 128), bf),
        in_specs=[pl.BlockSpec(memory_space=pltpu.VMEM)] * 2,
        out_specs=pl.BlockSpec(memory_space=pltpu.VMEM),
        scratch_shapes=[pltpu.VMEM((1024, 128), f32)],
        cost_estimate=pl.CostEstimate(flops=4 * 10**9, bytes_accessed=10**7, transcendentals=0),
    )(index, m)


def halo(x, axes):
    devices = lax.axis_size(axes)
    odd = lax.axis_index(axes) % 2 == 1
    leading, last = x[:, :HALO], x[:, x.shape[1] - HALO :]
    first = [(i, i ^ 1) for i in range(devices)]
    second = [(i, i + 1) for i in range(1, devices - 1, 2)]
    second += [(j, i) for i, j in second]
    one = lax.ppermute(jnp.where(odd, leading, last), axes, first)
    two = lax.ppermute(jnp.where(odd, last, leading), axes, second)
    return jnp.where(odd, one, two), jnp.where(odd, two, one)


def body(multipoles, translations, send_index, far_slots, far_types, near_list, particles):
    axes = ("gx", "gy", "gz")
    devices = send_index.shape[1]
    mine = jnp.transpose(particles, (1, 0, 2))
    before, after = halo(mine, axes)
    outgoing = pick(send_index[0].T, multipoles)
    incoming = lax.all_to_all(outgoing, axes, split_axis=0, concat_axis=0, tiled=True)
    entries = (far_slots + devices * CAP * far_types).reshape(16, NLF * NL // 16)
    speeds = near(near_list, before, mine, after)
    expansion = far(entries, incoming, translations)
    return (expansion, jnp.transpose(speeds, (1, 0, 2)))


def solution(mesh):
    placed = (
        P(("gx", "gy", "gz"), None),
        P(),
        P(("gx", "gy", "gz"), None, None),
        P(("gx", "gy", "gz"), None),
        P(("gx", "gy", "gz"), None),
        P(("gx", "gy", "gz"), None),
        P(("gx", "gy", "gz"), None, None),
    )
    return jax.shard_map(
        body,
        mesh=mesh,
        in_specs=placed,
        out_specs=(P(("gx", "gy", "gz"), None), P(("gx", "gy", "gz"), None, None)),
        check_vma=False,
    )
```

```python
import functools
import math

import jax
import jax.numpy as jnp
from jax import lax
from jax.experimental import pallas as pl
from jax.experimental.pallas import tpu as pltpu
from jax.sharding import PartitionSpec as P

Q = 256
P_SIZE = 128
NT = 16
NL = 16
NN = 8
CAP = 2
HALO = 16
EPS2 = 0.25
NLF = 256
NE = NLF + 2 * HALO
UNROLL = 16
BLOCKS = 8
bf = jnp.bfloat16
f32 = jnp.float32


def split3(v):
    a=v.astype(bf).astype(f32); r=v-a
    b=r.astype(bf).astype(f32)
    return a,b,r-b

def near_kernel(near_hbm, before_ref, mine_hbm, after_ref, out_ref, tgt, bt, gb, wa, wb, acc, mine_ref, near_ref, sems, *, U, PU):
    copies=[pltpu.make_async_copy(mine_hbm,mine_ref,sems.at[0]),pltpu.make_async_copy(near_hbm,near_ref,sems.at[1])]
    for copy in copies: copy.start()
    rows=lax.broadcasted_iota(jnp.int32,(8,128),0)
    lane=lax.broadcasted_iota(jnp.int32,(1,128),1)
    z8=jnp.zeros((8,128),f32)
    lo3=rows<3; lo6=rows<6; is6=rows==6
    is0=(rows==0)|(rows==3); is1=(rows==1)|(rows==4)
    keep=[((lane>=32*v)&(lane<32*v+32)).astype(f32).astype(bf) for v in range(4)]
    is7=rows==7; end=lo3|is7
    scale_t=jnp.where(lo6,-2.0,jnp.where(is6,0.0,1.0)); fixed_t=jnp.where(is6,1.0,0.0)
    def one(ref,e,eg):
        y=[jnp.broadcast_to(ref[c,pl.ds(e,1),:],(8,128)) for c in range(6)]
        y,f=y[:3],y[3:]
        n=y[0]*y[0]+y[1]*y[1]+y[2]*y[2]
        a=y[0]*f[0]+y[1]*f[1]+y[2]*f[2]
        Q=jnp.where(is0,y[0],jnp.where(is1,y[1],y[2]))
        F=jnp.where(is0,f[0],jnp.where(is1,f[1],f[2]))
        t0=jnp.where(lo3,n*F+a*Q,jnp.where(lo6,F,jnp.where(is6,a,y[2]*f[2])))
        t1=jnp.where(lo3,y[0],jnp.where(lo6,y[1],y[2]))*jnp.where(lo6,F,jnp.where(is6,f[0],f[1]))
        t=jnp.concatenate([t0,t1],axis=0)
        g1=t.astype(bf)
        g2=(t-g1.astype(f32)).astype(bf)
        gb[eg]=jnp.concatenate([g1,g2],axis=0)
        q1,q2,q3=split3(jnp.where(lo6,Q,jnp.where(is6,n+EPS2,n)))
        src=jnp.concatenate([jnp.where(is7,1.0,q1),jnp.where(is7,1.0,jnp.where(lo3,q1,q2)),jnp.where(is7,1.0,jnp.where(lo3,q2,q3)),z8],axis=0)
        if ref is mine_ref:
            tg=[jnp.where(end,q1,q2),jnp.where(lo3,q3,jnp.where(is7,q2,q1)),jnp.where(lo3,q2,jnp.where(is7,q3,q1))]
            tgt[e]=jnp.concatenate([v*scale_t+fixed_t for v in tg]+[z8],axis=0).astype(bf)
        return src.astype(bf)
    def prep(ref,base,n,un):
        def four(i,_):
            for w in range(un):
                o=(i*un+w)*4
                B=jnp.concatenate([one(ref,o+v,base+o+v) for v in range(4)],axis=0).T
                for v in range(4):
                    bt[base+o+v]=B*keep[v]
            return 0
        lax.fori_loop(0,n//(4*un),four,0)
    prep(before_ref,0,16,4); prep(after_ref,272,16,4)
    for copy in copies: copy.wait()
    prep(mine_ref,16,256,PU)
    Z=jnp.zeros((128,128),bf)
    def stage1(l,w,u):
        A4,B4=[jnp.concatenate([tgt[l+j]]*4,axis=0) for j in range(2)]
        R=jnp.concatenate([jnp.concatenate([A4,Z],axis=1),jnp.concatenate([Z,B4],axis=1)],axis=0)
        D=[jnp.concatenate([bt[near_ref[k,l+j]] for j in range(2)],axis=1) for k in range(NN)]
        s=jnp.dot(jnp.concatenate(D,axis=0),R,preferred_element_type=f32)
        v=lax.rsqrt(s)
        w3=(v*v*v).astype(bf)
        for j in range(2):
            w[u+j]=w3[:,j*128:j*128+128]
    def stage2(l,w,u):
        G=jnp.concatenate([gb[near_ref[k,l]] for k in range(NN)],axis=1)
        T=jnp.dot(G,w[u],preferred_element_type=f32)
        acc[pl.ds(pl.multiple_of(l*16,16),16),:]=T[0:16]+T[16:32]
    for u in range(0,U,2): stage1(u,wa,u)
    scale=1.0/(8.0*math.pi)
    def fin(g,_):
        x=[mine_ref[c,pl.ds(g*8,8),:] for c in range(3)]
        t=[acc[pl.ds(g*8*16+r,8,stride=16),:] for r in range(16)]
        n=x[0]*x[0]+x[1]*x[1]+x[2]*x[2]+2*EPS2
        N=t[0:3]; F=t[3:6]; A=t[6]
        Ym=[t[8:11],t[11:14],[t[14],t[15],t[7]]]
        xf=x[0]*F[0]+x[1]*F[1]+x[2]*F[2]-A
        for c in range(3):
            v=n*F[c]+N[c]+x[c]*xf
            for b in range(3):
                v=v-x[b]*(2.0*Ym[b][c]+Ym[c][b])
            out_ref[c,pl.ds(g*8,8),:]=v*scale
        return 0
    def it(i,_):
        b=i*2*U
        for u in range(0,U,2):
            if u%8==0: fin(jnp.maximum(i-1,0)*(2*U//8)+u//8,0)
            stage2(b+u,wa,u)
            stage1(b+U+u,wb,u)
            stage2(b+u+1,wa,u+1)
        for u in range(0,U,2):
            if u%8==0: fin(jnp.maximum(i-1,0)*(2*U//8)+U//8+u//8,0)
            stage2(b+U+u,wb,u)
            stage1(jnp.minimum(b+2*U+u,NLF-2),wa,u)
            stage2(b+U+u+1,wb,u+1)
        return 0
    lax.fori_loop(0,NLF//(2*U),it,0)
    for j in range(2*U//8): fin(NLF//8-2*U//8+j,0)

def near(near_list, before, mine, after):
    return pl.pallas_call(
        functools.partial(near_kernel, U=UNROLL, PU=8),
        out_shape=jax.ShapeDtypeStruct((3, NLF, P_SIZE), f32),
        in_specs=[pl.BlockSpec(memory_space=m) for m in (pltpu.HBM, pltpu.VMEM, pltpu.HBM, pltpu.VMEM)],
        out_specs=pl.BlockSpec(memory_space=pltpu.VMEM),
        scratch_shapes=[
            pltpu.VMEM((NLF, 32, 128), bf),
            pltpu.VMEM((NE, 128, 128), bf),
            pltpu.VMEM((NE, 32, 128), bf),
            pltpu.VMEM((UNROLL, 1024, 128), bf),
            pltpu.VMEM((UNROLL, 1024, 128), bf),
            pltpu.VMEM((NLF * 16, 128), f32),
            pltpu.VMEM((6, NLF, 128), f32),
            pltpu.SMEM((NN, NLF), jnp.int32),
            pltpu.SemaphoreType.DMA((2,)),
        ],
        compiler_params=pltpu.CompilerParams(vmem_limit_bytes=32 * 2**20),
        cost_estimate=pl.CostEstimate(flops=60 * 10**9, bytes_accessed=2 * 10**6, transcendentals=33 * 10**6),
    )(near_list.T, before, mine, after)


def far_kernel(enc_ref, r_ref, t_ref, out_ref, g_ref, s_ref):
    s_ref[...] = r_ref[...].reshape(1024, 128).astype(f32)
    table = jnp.concatenate([s_ref[pl.ds(h, 512, stride=2), :] for h in range(2)], axis=1).astype(bf)
    sub = lax.broadcasted_iota(jnp.int32, (256, 256), 0)
    leaf = lax.broadcasted_iota(jnp.int32, (1, 256), 1) // NL
    lane = lax.broadcasted_iota(jnp.int32, (1, 512), 1).astype(f32)
    def picks(b):
        e = enc_ref[pl.ds(b, 1), :]
        slot = (e & 511).astype(f32)
        cls = (e >> 9) * 16 + leaf
        col = jnp.concatenate([jnp.broadcast_to(slot[:, h * 128 : h * 128 + 128], (128, 128)).T for h in range(2)], axis=0)
        col = jnp.concatenate([col] * 4, axis=1)
        pick = (col == lane).astype(f32).astype(bf)
        own = (sub == cls).astype(f32).astype(bf)
        return pick, own
    def block(i, _):
        both = [picks(i * BLOCKS + j) for j in range(BLOCKS)]
        rows = jnp.dot(jnp.concatenate([p for p, _ in both], axis=0), table, preferred_element_type=f32).astype(bf)
        for j in range(BLOCKS):
            g = jnp.dot(both[j][1], rows[j * 256 : j * 256 + 256], preferred_element_type=f32).astype(bf)
            b = pl.multiple_of((i * BLOCKS + j) * 16, 16)
            for t in range(NT):
                g_ref[pl.ds(b, 16), t * Q : t * Q + Q] = g[t * 16 : t * 16 + 16]
        return 0
    lax.fori_loop(0, 16 // BLOCKS, block, 0)
    out_ref[...] = jnp.dot(g_ref[...], t_ref[...].reshape(NT * Q, Q), preferred_element_type=f32)


def far(enc, received, translations):
    return pl.pallas_call(far_kernel, out_shape=jax.ShapeDtypeStruct((256,Q),f32),
        in_specs=[pl.BlockSpec(memory_space=pltpu.VMEM)]*3, out_specs=pl.BlockSpec(memory_space=pltpu.VMEM),
        scratch_shapes=[pltpu.VMEM((256,NT*Q),bf), pltpu.VMEM((1024,128),f32)],
        compiler_params=pltpu.CompilerParams(vmem_limit_bytes=24*2**20))(enc,received,translations)


def pick_kernel(i_ref, m_ref, out_ref, rows_ref):
    lane = lax.broadcasted_iota(jnp.int32, (1, 256), 1).astype(f32)
    for c in range(2):
        index = i_ref[c : c + 1, :].astype(f32)
        col = jnp.concatenate([jnp.broadcast_to(index[:, h * 128 : h * 128 + 128], (128, 128)).T for h in range(2)], axis=0)
        pick = (jnp.concatenate([col, col], axis=1) == lane).astype(f32).astype(bf)
        got = jnp.dot(pick, m_ref[...], preferred_element_type=f32)
        for h in range(2):
            rows_ref[pl.ds(2 * c + h, 256, stride=4), :] = got[:, h * 128 : h * 128 + 128]
    out_ref[...] = rows_ref[...].astype(bf).reshape(256, 4, 128)


def pick(index, m):
    return pl.pallas_call(
        pick_kernel,
        out_shape=jax.ShapeDtypeStruct((256, 4, 128), bf),
        in_specs=[pl.BlockSpec(memory_space=pltpu.VMEM)] * 2,
        out_specs=pl.BlockSpec(memory_space=pltpu.VMEM),
        scratch_shapes=[pltpu.VMEM((1024, 128), f32)],
        cost_estimate=pl.CostEstimate(flops=4 * 10**9, bytes_accessed=10**7, transcendentals=0),
    )(index, m)


def halo(x, axes):
    devices = lax.axis_size(axes)
    odd = lax.axis_index(axes) % 2 == 1
    leading, last = x[:, :HALO], x[:, x.shape[1] - HALO :]
    first = [(i, i ^ 1) for i in range(devices)]
    second = [(i, i + 1) for i in range(1, devices - 1, 2)]
    second += [(j, i) for i, j in second]
    one = lax.ppermute(jnp.where(odd, leading, last), axes, first)
    two = lax.ppermute(jnp.where(odd, last, leading), axes, second)
    return jnp.where(odd, one, two), jnp.where(odd, two, one)


def body(multipoles, translations, send_index, far_slots, far_types, near_list, particles):
    axes = ("gx", "gy", "gz")
    devices = send_index.shape[1]
    mine = jnp.transpose(particles, (1, 0, 2))
    before, after = halo(mine, axes)
    outgoing = pick(send_index[0].T, multipoles)
    incoming = lax.all_to_all(outgoing, axes, split_axis=0, concat_axis=0, tiled=True)
    entries = (far_slots + devices * CAP * far_types).reshape(16, NLF * NL // 16)
    speeds = near(near_list, before, mine, after)
    expansion = far(entries, incoming, translations)
    return (expansion, jnp.transpose(speeds, (1, 0, 2)))


def solution(mesh):
    placed = (
        P(("gx", "gy", "gz"), None),
        P(),
        P(("gx", "gy", "gz"), None, None),
        P(("gx", "gy", "gz"), None),
        P(("gx", "gy", "gz"), None),
        P(("gx", "gy", "gz"), None),
        P(("gx", "gy", "gz"), None, None),
    )
    return jax.shard_map(
        body,
        mesh=mesh,
        in_specs=placed,
        out_specs=(P(("gx", "gy", "gz"), None), P(("gx", "gy", "gz"), None, None)),
        check_vma=False,
    )
```

```python
import functools
import math

import jax
import jax.numpy as jnp
from jax import lax
from jax.experimental import pallas as pl
from jax.experimental.pallas import tpu as pltpu
from jax.sharding import PartitionSpec as P

Q = 256
P_SIZE = 128
NT = 16
NL = 16
NN = 8
CAP = 2
HALO = 16
EPS2 = 0.25
NLF = 256
NE = NLF + 2 * HALO
UNROLL = 32
BLOCKS = 8
bf = jnp.bfloat16
f32 = jnp.float32


def split3(v):
    a=v.astype(bf).astype(f32); r=v-a
    b=r.astype(bf).astype(f32)
    return a,b,r-b

def near_kernel(near_hbm, before_ref, mine_hbm, after_ref, out_ref, tgt, bt, gb, wa, wb, acc, mine_ref, near_ref, sems, *, U, PU):
    copies=[pltpu.make_async_copy(mine_hbm,mine_ref,sems.at[0]),pltpu.make_async_copy(near_hbm,near_ref,sems.at[1])]
    for copy in copies: copy.start()
    rows=lax.broadcasted_iota(jnp.int32,(8,128),0)
    lane=lax.broadcasted_iota(jnp.int32,(1,128),1)
    z8=jnp.zeros((8,128),f32)
    lo3=rows<3; lo6=rows<6; is6=rows==6
    is0=(rows==0)|(rows==3); is1=(rows==1)|(rows==4)
    keep=[((lane>=32*v)&(lane<32*v+32)).astype(f32).astype(bf) for v in range(4)]
    is7=rows==7; end=lo3|is7
    scale_t=jnp.where(lo6,-2.0,jnp.where(is6,0.0,1.0)); fixed_t=jnp.where(is6,1.0,0.0)
    def one(ref,e,eg):
        y=[jnp.broadcast_to(ref[c,pl.ds(e,1),:],(8,128)) for c in range(6)]
        y,f=y[:3],y[3:]
        n=y[0]*y[0]+y[1]*y[1]+y[2]*y[2]
        a=y[0]*f[0]+y[1]*f[1]+y[2]*f[2]
        Q=jnp.where(is0,y[0],jnp.where(is1,y[1],y[2]))
        F=jnp.where(is0,f[0],jnp.where(is1,f[1],f[2]))
        t0=jnp.where(lo3,n*F+a*Q,jnp.where(lo6,F,jnp.where(is6,a,y[2]*f[2])))
        t1=jnp.where(lo3,y[0],jnp.where(lo6,y[1],y[2]))*jnp.where(lo6,F,jnp.where(is6,f[0],f[1]))
        t=jnp.concatenate([t0,t1],axis=0)
        g1=t.astype(bf)
        g2=(t-g1.astype(f32)).astype(bf)
        gb[eg]=jnp.concatenate([g1,g2],axis=0)
        q1,q2,q3=split3(jnp.where(lo6,Q,jnp.where(is6,n+EPS2,n)))
        src=jnp.concatenate([jnp.where(is7,1.0,q1),jnp.where(is7,1.0,jnp.where(lo3,q1,q2)),jnp.where(is7,1.0,jnp.where(lo3,q2,q3)),z8],axis=0)
        if ref is mine_ref:
            tg=[jnp.where(end,q1,q2),jnp.where(lo3,q3,jnp.where(is7,q2,q1)),jnp.where(lo3,q2,jnp.where(is7,q3,q1))]
            tgt[e]=jnp.concatenate([v*scale_t+fixed_t for v in tg]+[z8],axis=0).astype(bf)
        return src.astype(bf)
    def prep(ref,base,n,un):
        def four(i,_):
            for w in range(un):
                o=(i*un+w)*4
                B=jnp.concatenate([one(ref,o+v,base+o+v) for v in range(4)],axis=0).T
                for v in range(4):
                    bt[base+o+v]=B*keep[v]
            return 0
        lax.fori_loop(0,n//(4*un),four,0)
    prep(before_ref,0,16,4); prep(after_ref,272,16,4)
    for copy in copies: copy.wait()
    prep(mine_ref,16,256,PU)
    Z=jnp.zeros((128,128),bf)
    def stage1(l,w,u):
        A4,B4=[jnp.concatenate([tgt[l+j]]*4,axis=0) for j in range(2)]
        R=jnp.concatenate([jnp.concatenate([A4,Z],axis=1),jnp.concatenate([Z,B4],axis=1)],axis=0)
        D=[jnp.concatenate([bt[near_ref[k,l+j]] for j in range(2)],axis=1) for k in range(NN)]
        s=jnp.dot(jnp.concatenate(D,axis=0),R,preferred_element_type=f32)
        v=lax.rsqrt(s)
        w3=(v*v*v).astype(bf)
        for j in range(2):
            w[u+j]=w3[:,j*128:j*128+128]
    def stage2(l,w,u):
        G=jnp.concatenate([gb[near_ref[k,l]] for k in range(NN)],axis=1)
        T=jnp.dot(G,w[u],preferred_element_type=f32)
        acc[pl.ds(pl.multiple_of(l*16,16),16),:]=T[0:16]+T[16:32]
    for u in range(0,U,2): stage1(u,wa,u)
    scale=1.0/(8.0*math.pi)
    def fin(g,_):
        x=[mine_ref[c,pl.ds(g*8,8),:] for c in range(3)]
        t=[acc[pl.ds(g*8*16+r,8,stride=16),:] for r in range(16)]
        n=x[0]*x[0]+x[1]*x[1]+x[2]*x[2]+2*EPS2
        N=t[0:3]; F=t[3:6]; A=t[6]
        Ym=[t[8:11],t[11:14],[t[14],t[15],t[7]]]
        xf=x[0]*F[0]+x[1]*F[1]+x[2]*F[2]-A
        for c in range(3):
            v=n*F[c]+N[c]+x[c]*xf
            for b in range(3):
                v=v-x[b]*(2.0*Ym[b][c]+Ym[c][b])
            out_ref[c,pl.ds(g*8,8),:]=v*scale
        return 0
    def it(i,_):
        b=i*2*U
        for u in range(0,U,2):
            if u%8==0: fin(jnp.maximum(i-1,0)*(2*U//8)+u//8,0)
            stage2(b+u,wa,u)
            stage1(b+U+u,wb,u)
            stage2(b+u+1,wa,u+1)
        for u in range(0,U,2):
            if u%8==0: fin(jnp.maximum(i-1,0)*(2*U//8)+U//8+u//8,0)
            stage2(b+U+u,wb,u)
            stage1(jnp.minimum(b+2*U+u,NLF-2),wa,u)
            stage2(b+U+u+1,wb,u+1)
        return 0
    lax.fori_loop(0,NLF//(2*U),it,0)
    for j in range(2*U//8): fin(NLF//8-2*U//8+j,0)

def near(near_list, before, mine, after):
    return pl.pallas_call(
        functools.partial(near_kernel, U=UNROLL, PU=8),
        out_shape=jax.ShapeDtypeStruct((3, NLF, P_SIZE), f32),
        in_specs=[pl.BlockSpec(memory_space=m) for m in (pltpu.HBM, pltpu.VMEM, pltpu.HBM, pltpu.VMEM)],
        out_specs=pl.BlockSpec(memory_space=pltpu.VMEM),
        scratch_shapes=[
            pltpu.VMEM((NLF, 32, 128), bf),
            pltpu.VMEM((NE, 128, 128), bf),
            pltpu.VMEM((NE, 32, 128), bf),
            pltpu.VMEM((UNROLL, 1024, 128), bf),
            pltpu.VMEM((UNROLL, 1024, 128), bf),
            pltpu.VMEM((NLF * 16, 128), f32),
            pltpu.VMEM((6, NLF, 128), f32),
            pltpu.SMEM((NN, NLF), jnp.int32),
            pltpu.SemaphoreType.DMA((2,)),
        ],
        compiler_params=pltpu.CompilerParams(vmem_limit_bytes=44 * 2**20),
        cost_estimate=pl.CostEstimate(flops=60 * 10**9, bytes_accessed=2 * 10**6, transcendentals=33 * 10**6),
    )(near_list.T, before, mine, after)


def far_kernel(enc_ref, r_ref, t_ref, out_ref, g_ref, s_ref):
    s_ref[...] = r_ref[...].reshape(1024, 128).astype(f32)
    table = jnp.concatenate([s_ref[pl.ds(h, 512, stride=2), :] for h in range(2)], axis=1).astype(bf)
    sub = lax.broadcasted_iota(jnp.int32, (256, 256), 0)
    leaf = lax.broadcasted_iota(jnp.int32, (1, 256), 1) // NL
    lane = lax.broadcasted_iota(jnp.int32, (1, 512), 1).astype(f32)
    def picks(b):
        e = enc_ref[pl.ds(b, 1), :]
        slot = (e & 511).astype(f32)
        cls = (e >> 9) * 16 + leaf
        col = jnp.concatenate([jnp.broadcast_to(slot[:, h * 128 : h * 128 + 128], (128, 128)).T for h in range(2)], axis=0)
        col = jnp.concatenate([col] * 4, axis=1)
        pick = (col == lane).astype(f32).astype(bf)
        own = (sub == cls).astype(f32).astype(bf)
        return pick, own
    def block(i, _):
        both = [picks(i * BLOCKS + j) for j in range(BLOCKS)]
        rows = jnp.dot(jnp.concatenate([p for p, _ in both], axis=0), table, preferred_element_type=f32).astype(bf)
        for j in range(BLOCKS):
            g = jnp.dot(both[j][1], rows[j * 256 : j * 256 + 256], preferred_element_type=f32).astype(bf)
            b = pl.multiple_of((i * BLOCKS + j) * 16, 16)
            for t in range(NT):
                g_ref[pl.ds(b, 16), t * Q : t * Q + Q] = g[t * 16 : t * 16 + 16]
        return 0
    lax.fori_loop(0, 16 // BLOCKS, block, 0)
    out_ref[...] = jnp.dot(g_ref[...], t_ref[...].reshape(NT * Q, Q), preferred_element_type=f32)


def far(enc, received, translations):
    return pl.pallas_call(far_kernel, out_shape=jax.ShapeDtypeStruct((256,Q),f32),
        in_specs=[pl.BlockSpec(memory_space=pltpu.VMEM)]*3, out_specs=pl.BlockSpec(memory_space=pltpu.VMEM),
        scratch_shapes=[pltpu.VMEM((256,NT*Q),bf), pltpu.VMEM((1024,128),f32)],
        compiler_params=pltpu.CompilerParams(vmem_limit_bytes=24*2**20))(enc,received,translations)


def pick_kernel(i_ref, m_ref, out_ref, rows_ref):
    lane = lax.broadcasted_iota(jnp.int32, (1, 256), 1).astype(f32)
    for c in range(2):
        index = i_ref[c : c + 1, :].astype(f32)
        col = jnp.concatenate([jnp.broadcast_to(index[:, h * 128 : h * 128 + 128], (128, 128)).T for h in range(2)], axis=0)
        pick = (jnp.concatenate([col, col], axis=1) == lane).astype(f32).astype(bf)
        got = jnp.dot(pick, m_ref[...], preferred_element_type=f32)
        for h in range(2):
            rows_ref[pl.ds(2 * c + h, 256, stride=4), :] = got[:, h * 128 : h * 128 + 128]
    out_ref[...] = rows_ref[...].astype(bf).reshape(256, 4, 128)


def pick(index, m):
    return pl.pallas_call(
        pick_kernel,
        out_shape=jax.ShapeDtypeStruct((256, 4, 128), bf),
        in_specs=[pl.BlockSpec(memory_space=pltpu.VMEM)] * 2,
        out_specs=pl.BlockSpec(memory_space=pltpu.VMEM),
        scratch_shapes=[pltpu.VMEM((1024, 128), f32)],
        cost_estimate=pl.CostEstimate(flops=4 * 10**9, bytes_accessed=10**7, transcendentals=0),
    )(index, m)


def halo(x, axes):
    devices = lax.axis_size(axes)
    odd = lax.axis_index(axes) % 2 == 1
    leading, last = x[:, :HALO], x[:, x.shape[1] - HALO :]
    first = [(i, i ^ 1) for i in range(devices)]
    second = [(i, i + 1) for i in range(1, devices - 1, 2)]
    second += [(j, i) for i, j in second]
    one = lax.ppermute(jnp.where(odd, leading, last), axes, first)
    two = lax.ppermute(jnp.where(odd, last, leading), axes, second)
    return jnp.where(odd, one, two), jnp.where(odd, two, one)


def body(multipoles, translations, send_index, far_slots, far_types, near_list, particles):
    axes = ("gx", "gy", "gz")
    devices = send_index.shape[1]
    mine = jnp.transpose(particles, (1, 0, 2))
    before, after = halo(mine, axes)
    outgoing = pick(send_index[0].T, multipoles)
    incoming = lax.all_to_all(outgoing, axes, split_axis=0, concat_axis=0, tiled=True)
    entries = (far_slots + devices * CAP * far_types).reshape(16, NLF * NL // 16)
    speeds = near(near_list, before, mine, after)
    expansion = far(entries, incoming, translations)
    return (expansion, jnp.transpose(speeds, (1, 0, 2)))


def solution(mesh):
    placed = (
        P(("gx", "gy", "gz"), None),
        P(),
        P(("gx", "gy", "gz"), None, None),
        P(("gx", "gy", "gz"), None),
        P(("gx", "gy", "gz"), None),
        P(("gx", "gy", "gz"), None),
        P(("gx", "gy", "gz"), None, None),
    )
    return jax.shard_map(
        body,
        mesh=mesh,
        in_specs=placed,
        out_specs=(P(("gx", "gy", "gz"), None), P(("gx", "gy", "gz"), None, None)),
        check_vma=False,
    )
```
